256 devices in a mesh: frame: 16 (over z_lo, y), patch: 16 (over z_hi, x, core).
Axes of the slice: x: 4, y: 4, z: 8 (z_hi: 2, z_lo: 4; z = z_hi * 4 + z_lo), core: 2. Of those that a mesh axis runs over, the one named last changes fastest.
Arguments:
- hidden_states: bfloat16 [16, 4096, 1152], P('frame', 'patch'), may hold values from -6 to 6
- mod_spatial: float32 [3, 1152], replicated, may hold values from -4 to 4
- w_spatial_qkv: bfloat16 [1152, 3456], P(None, 'patch'), may hold values from -2.5 to 2.5
- w_spatial_out: bfloat16 [1152, 1152], P('patch'), may hold values from -0.1875 to 0.1875
- mod_temporal: float32 [3, 1152], replicated, may hold values from -4 to 4
- w_temporal_qkv: bfloat16 [1152, 3456], P(None, 'frame'), may hold values from -2.5 to 2.5
- w_temporal_out: bfloat16 [1152, 1152], P('frame'), may hold values from -0.1875 to 0.1875
Outputs:
- block_out: bfloat16 [16, 4096, 1152], P('frame', 'patch')
The draws below stay inside these ranges and needn't reach their ends.
All inputs are finite; a program needn't handle non-finite values.
Results may differ from the reference program's by a relative error of at most 0.017.
Values may be sent and summed in bfloat16 or wider, within the bound.
A program may use at most 64 MiB of HBM per device.

```python
import math
import jax
import jax.numpy as jnp
from jax import lax

D = 1152
HEADS = 16
HEAD_DIM = 72
FRAMES = 16
PATCHES = 4096


def smooth_field(key):
    keys = jax.random.split(key, 3)
    along_frames = jax.random.randint(keys[0], (D,), 1, 4).astype(jnp.float32)
    along_patches = jax.random.randint(keys[1], (D,), 1, 5).astype(jnp.float32)
    phase = jax.random.uniform(keys[2], (D,), jnp.float32, -math.pi, math.pi)
    frame_pos = jnp.arange(FRAMES, dtype=jnp.float32)[:, None, None] / FRAMES
    patch_pos = jnp.arange(PATCHES, dtype=jnp.float32)[None, :, None] / PATCHES
    return jnp.cos(2.0 * math.pi * (along_frames * frame_pos + along_patches * patch_pos) + phase)


def draw_hidden_states(key, part):
    key = jax.random.fold_in(key, 11)
    keys = jax.random.split(key, 2)
    smooth = smooth_field(keys[0])
    noise = jax.random.normal(keys[1], (FRAMES, PATCHES, D), jnp.float32)
    base = 0.85 * noise + 0.5 * smooth
    return jnp.clip(base, -6.0, 6.0).astype(jnp.bfloat16)


def projection_draw(key, spread):
    keys = jax.random.split(key, 4)
    shape = (D, HEADS, 1, HEAD_DIM)
    query = jax.random.normal(keys[0], shape, jnp.float32) / math.sqrt(D)
    other = jax.random.normal(keys[1], shape, jnp.float32) / math.sqrt(D)
    value = jax.random.normal(keys[2], shape, jnp.float32) / math.sqrt(D)
    gains = jnp.exp(jax.random.uniform(keys[3], (1, HEADS, 1, 1), jnp.float32, 0.0, spread))
    whole = jnp.concatenate([gains * query, other, value], axis=2)
    return jnp.clip(whole, -2.5, 2.5).reshape(D, 3 * D)


def draw_w_spatial_qkv(key, part):
    key = jax.random.fold_in(key, 23)
    return projection_draw(key, 0.0).astype(jnp.bfloat16)


def draw_w_temporal_qkv(key, part):
    key = jax.random.fold_in(key, 37)
    return projection_draw(key, 0.0).astype(jnp.bfloat16)


def levels(own_key, extent, cuts, low, top_value):
    gain = 1.0
    for dim, blocks in cuts:
        heights = jax.random.uniform(jax.random.fold_in(jax.random.fold_in(own_key, 6), dim), (blocks,), jnp.float32, low / len(cuts), top_value / len(cuts))
        gain = gain * jnp.repeat(jnp.exp(heights), extent[dim] // blocks).reshape((-1,) + (1,) * (len(extent) - 1 - dim))
    return gain


def normal_values(key, shape, scale, bound, cuts=(), kind=jnp.bfloat16):
    entries = scale * jax.random.normal(key, shape, jnp.float32)
    if cuts:
        entries = entries * levels(key, shape, cuts, -0.22, 0.18)
    return jnp.clip(entries, -bound, bound).astype(kind)


def setup_inputs(seed: int = 0) -> dict:
    key_list = jax.random.split(jax.random.key(seed), 8)
    return {
        "hidden_states": draw_hidden_states(jax.random.fold_in(key_list[7], 71), 0),
        "mod_spatial": normal_values(key_list[1], (3, D), 0.7, 4.0, (), jnp.float32),
        "w_spatial_qkv": draw_w_spatial_qkv(jax.random.fold_in(key_list[7], 71), 0),
        "w_spatial_out": normal_values(key_list[3], (D, D), D ** -0.5, 0.1875, ((0, 16),)),
        "mod_temporal": normal_values(key_list[4], (3, D), 0.7, 4.0, (), jnp.float32),
        "w_temporal_qkv": draw_w_temporal_qkv(jax.random.fold_in(key_list[7], 71), 0),
        "w_temporal_out": normal_values(key_list[6], (D, D), D ** -0.5, 0.1875, ((0, 16),)),
    }


EPS = 1e-06

def modulate(tokens, mod):
    values = tokens.astype(jnp.float32)
    mean = lax.optimization_barrier(jnp.mean(values, axis=-1, keepdims=True))
    centred = values - mean
    var = lax.optimization_barrier(jnp.mean(centred * centred, axis=-1, keepdims=True))
    normed = centred * lax.rsqrt(var + EPS)
    return (normed * (1.0 + mod[1]) + mod[0]).astype(jnp.bfloat16)

def project_qkv(tokens, mod, weight):
    frames, patches, width = tokens.shape
    moved = modulate(tokens, mod).reshape(frames * patches, width)
    qkv = jnp.dot(moved, weight, preferred_element_type=jnp.float32).astype(jnp.bfloat16)
    return qkv.reshape(frames, patches, HEADS, 3, HEAD_DIM)

def spatial_frame(qkv):
    query = qkv[:, :, 0].astype(jnp.float32)
    keys = qkv[:, :, 1].astype(jnp.float32)
    values = qkv[:, :, 2].astype(jnp.float32)
    scores = jnp.einsum('qhd,khd->hqk', query, keys) / math.sqrt(HEAD_DIM)
    probs = jax.nn.softmax(scores, axis=-1).astype(jnp.bfloat16)
    return jnp.einsum('hqk,khd->qhd', probs.astype(jnp.float32), values).astype(jnp.bfloat16)

def temporal_all(qkv):
    query = qkv[:, :, :, 0].astype(jnp.float32)
    keys = qkv[:, :, :, 1].astype(jnp.float32)
    values = qkv[:, :, :, 2].astype(jnp.float32)
    scores = jnp.einsum('fphd,gphd->phfg', query, keys) / math.sqrt(HEAD_DIM)
    probs = jax.nn.softmax(scores, axis=-1).astype(jnp.bfloat16)
    return jnp.einsum('phfg,gphd->fphd', probs.astype(jnp.float32), values).astype(jnp.bfloat16)

def finish(tokens, heads, mod, weight):
    frames, patches, width = tokens.shape
    flat = heads.reshape(frames * patches, width)
    update = jnp.dot(flat, weight, preferred_element_type=jnp.float32).reshape(frames, patches, width)
    return (tokens.astype(jnp.float32) + mod[2] * update).astype(jnp.bfloat16)

def reference(hidden_states, mod_spatial, w_spatial_qkv, w_spatial_out, mod_temporal, w_temporal_qkv, w_temporal_out):
    qkv = project_qkv(hidden_states, mod_spatial, w_spatial_qkv)
    heads = lax.map(spatial_frame, qkv)
    after_spatial = finish(hidden_states, heads, mod_spatial, w_spatial_out)
    qkv = project_qkv(after_spatial, mod_temporal, w_temporal_qkv)
    heads = temporal_all(qkv)
    return finish(after_spatial, heads, mod_temporal, w_temporal_out)
```

```python
import functools
import math

import jax
import jax.numpy as jnp
from jax import lax
from jax.experimental import pallas as pl
from jax.experimental.pallas import tpu as pltpu
from jax.sharding import PartitionSpec as P

HEADS = 16
HEAD_DIM = 72
EPS = 1e-06
MESH = pl.DeviceIdType.MESH
Q_SCALE = math.log2(math.e) / math.sqrt(HEAD_DIM)
LOW = -1e30
N_COPIES = 160


def dot(a, b, ca, cb):
    return lax.dot_general(a, b, (((ca,), (cb,)), ((), ())), preferred_element_type=jnp.float32)


def modulate(tokens, mod_ref):
    values = tokens.astype(jnp.float32)
    mean = jnp.mean(values, axis=-1, keepdims=True)
    centred = values - mean
    var = jnp.mean(centred * centred, axis=-1, keepdims=True)
    normed = centred * lax.rsqrt(var + EPS)
    return (normed * (1.0 + mod_ref[1:2, :]) + mod_ref[0:1, :]).astype(jnp.bfloat16)


def kernel(
    hid_ref, mod_s_ref, mod_t_ref, w_s_ref, w_t_ref, out_ref,
    tok_a, tok_b, wsp, wso, wt, wto, q_buf, k_buf, v_buf, acc, top, o_send, o_recv,
    t_send, t_recv, r_send, heads_t, send_sem, recv_sem,
):
    frame = lax.axis_index("frame")
    patch = lax.axis_index("patch")
    zlo, y = frame // 4, lax.rem(frame, 4)
    zhi, x, c = patch // 8, lax.rem(patch // 2, 4), lax.rem(patch, 2)
    z = zhi * 4 + zlo
    slot = x * 2 + c

    def device(z_=z, y_=y, x_=x, c_=c):
        return (lax.rem(z_, 4) * 4 + y_, (z_ // 4) * 8 + x_ * 2 + c_)

    def turn(value, step, size):
        return lax.rem(value + step + size, size)

    right, left = device(x_=turn(x, 1, 4)), device(x_=turn(x, -1, 4))
    sibling = device(c_=1 - c)
    partner = device(z_=turn(z, 4, 8))
    x_slots = [turn(x, d, 4) * 2 + c for d in range(4)]
    sib_slots = [turn(x, d, 4) * 2 + 1 - c for d in range(4)]

    barrier = pltpu.get_barrier_semaphore()
    greet = [device(x_=turn(x, d // 2, 4), c_=turn(c, d % 2, 2)) for d in range(1, 8)]
    greet += [(turn(frame, d, 16), patch) for d in range(1, 16)]
    greet += [device(z_=turn(z, d, 8)) for d in (4, 1, -1, 2, -2)]
    for other in greet:
        pl.semaphore_signal(barrier, inc=1, device_id=other, device_id_type=MESH)

    count = [0]
    sends = []

    class Move:
        def __init__(self, src, dst, target, landing=None, recv_id=None):
            self.i = count[0]
            count[0] += 1
            self.r = self.i if recv_id is None else recv_id
            self.args = (src, dst, target)
            self.landing = dst if landing is None else landing

        def desc(self, dst):
            src, _, target = self.args
            return pltpu.make_async_remote_copy(
                src_ref=src, dst_ref=dst, send_sem=send_sem.at[self.i],
                recv_sem=recv_sem.at[self.r], device_id=target, device_id_type=MESH,
            )

        def start(self):
            self.desc(self.args[1]).start()
            sends.append(self)

        def wait_recv(self):
            landing = self.landing
            pltpu.make_async_remote_copy(
                src_ref=landing, dst_ref=landing, send_sem=send_sem.at[self.i],
                recv_sem=recv_sem.at[self.r], device_id=self.args[2], device_id_type=MESH,
            ).wait_recv()

        def wait_send(self):
            self.desc(self.args[1]).wait_send()

    def start(*moves):
        for m in moves:
            m.start()

    def recv(*moves):
        for m in moves:
            m.wait_recv()

    class Ring:
        def __init__(self, buf, rows, cut):
            me, near, far, back = [buf.at[s] for s in x_slots]
            self.to_right = Move(me, me, right, back)
            self.to_left = Move(me, me, left, near)
            top_half, low_half = pl.ds(0, cut), pl.ds(cut, rows - cut)
            self.on_right = Move(back.at[top_half], back.at[top_half], right, far.at[top_half])
            self.on_left = Move(near.at[low_half], near.at[low_half], left, far.at[low_half])
            self.sib = [Move(buf.at[x_slots[d]], buf.at[x_slots[d]], sibling, buf.at[sib_slots[d]]) for d in range(4)]

        def begin(self):
            start(self.to_right, self.to_left, self.sib[0])

        def forward(self):
            recv(self.to_right)
            start(self.on_right)
            recv(self.to_left)
            start(self.on_left, self.sib[3], self.sib[1])

        def last(self):
            recv(self.on_right, self.on_left)
            start(self.sib[2])

        def done(self):
            recv(*self.sib)

    rings = [Ring(tok_a.at[n], 128, 64) for n in range(2)] + [Ring(tok_b.at[n], 64, 32) for n in range(4)]
    to_partner = [
        Move(tok_a.at[n // 2, slot, pl.ds((n % 2) * 64, 64)], tok_b.at[n, slot], partner) for n in range(4)
    ]
    wso_ring = Ring(wso, 144, 64)

    edge = jnp.logical_or(zlo == 0, zlo == 3)
    ahead = jnp.where(zlo == 0, -1, 1)
    cross_src = wsp.at[0, y]
    cross_dst = wsp.at[1, y]
    cross_near = Move(cross_src, cross_dst, device(z_=turn(z, ahead, 8)))
    cross_far = Move(cross_src, cross_dst, device(z_=turn(z, 2 * ahead, 8)), recv_id=cross_near.r)
    share = [
        Move(cross_dst, cross_dst, device(y_=turn(y, d, 4)), wsp.at[1, turn(y, -d, 4)]) for d in (1, 3, 2)
    ]

    def wt_slot(dz, dy):
        return turn(zlo, dz, 4) * 4 + turn(y, dy, 4)

    def wt_half(dz, dy):
        return wt.at[wt_slot(dz, dy), c]

    two = jnp.where(c == 0, 2, -2)
    z_moves = [
        Move(wt_half(0, 0), wt_half(0, 0), device(z_=turn(z, 1, 8)), wt_half(-1, 0)),
        Move(wt_half(0, 0), wt_half(0, 0), device(z_=turn(z, -1, 8)), wt_half(1, 0)),
        Move(wt_half(0, 0), wt_half(0, 0), device(z_=turn(z, two, 8)), wt_half(2, 0)),
    ]
    y_up, y_down = device(y_=turn(y, 1, 4)), device(y_=turn(y, -1, 4))

    class YRing:
        def __init__(self, dz):
            me, near, far, back = [wt_half(dz, d) for d in range(4)]
            self.up = Move(me, me, y_up, back)
            self.down = Move(me, me, y_down, near)
            first, second = pl.ds(0, 64), pl.ds(64, 80)
            self.on_up = Move(back.at[first], back.at[first], y_up, far.at[first])
            self.on_down = Move(near.at[second], near.at[second], y_down, far.at[second])
            self.sib = [
                Move(wt_half(dz, d), wt_half(dz, d), sibling, wt.at[wt_slot(dz, d), 1 - c])
                for d in range(4) if (dz, d) != (0, 0)
            ]

        def begin(self):
            start(self.up, self.down)
            if len(self.sib) == 4:
                start(self.sib[0])

        def forward(self):
            recv(self.up)
            start(self.on_up)
            recv(self.down)
            start(self.on_down, self.sib[-1], self.sib[-3])

        def last(self):
            recv(self.on_up, self.on_down)
            start(self.sib[-2])

        def done(self):
            recv(*self.sib)

    y_rings = {dz: YRing(dz) for dz in (0, 3, 1, 2)}

    def project(heads, tokens, q_at, k_at):
        n = tokens.shape[0]
        for h in heads:
            qkv = dot(wsp[h].reshape(320, 1152)[0:224], tokens, 1, 1)
            if q_at is not None:
                q = jnp.concatenate([qkv[0:72] * Q_SCALE, jnp.zeros((8, n), jnp.float32)], axis=0)
                q_buf[h, :, pl.ds(q_at, n)] = q.astype(jnp.bfloat16)
            k = jnp.concatenate([qkv[72:144], jnp.zeros((8, n), jnp.float32)], axis=0)
            k_buf[h, pl.ds(k_at, n), :] = k.T.astype(jnp.bfloat16)
            row = lax.broadcasted_iota(jnp.int32, (8, n), 0)
            one = jnp.where(row == 0, 1.0, 0.0)
            v_buf[h, :, pl.ds(k_at, n)] = jnp.concatenate([qkv[144:216], one], axis=0).astype(jnp.bfloat16)

    def flash(h, q_at, q_n, k_at, k_n):
        qs, ks = pl.ds(q_at, q_n), pl.ds(k_at, k_n)
        s = dot(k_buf[h, ks, :], q_buf[h, :, qs], 1, 0)
        before = top[h, 0:1, qs]
        now = jnp.maximum(before, jnp.max(s, axis=0, keepdims=True))
        p = jnp.exp2(s - now).astype(jnp.bfloat16)
        acc[h, :, qs] = acc[h, :, qs] * jnp.exp2(before - now) + dot(v_buf[h, :, ks], p, 1, 0)
        top[h, 0:1, qs] = now

    def own_tokens(n):
        return tok_a[n].reshape(1024, 1152)

    def far_tokens(n):
        return tok_b[n].reshape(512, 1152)

    moved = modulate(hid_ref[...], mod_s_ref)
    tok_a[0, slot] = moved[0:128]
    tok_a[1, slot] = moved[128:256]
    wsp[0] = w_s_ref[...].reshape(4, 80, 1152)
    wt[frame] = w_t_ref[...].reshape(2, 144, 1152)
    acc[...] = jnp.zeros_like(acc)
    top[...] = jnp.full_like(top, LOW)
    pl.semaphore_wait(barrier, len(greet))

    rings[0].begin()

    @pl.when(edge)
    def _():
        cross_near.start()
        cross_far.start()

    start(to_partner[0], to_partner[1])
    rings[1].begin()
    recv(cross_near)
    start(*share)
    rings[0].forward()
    y_rings[0].begin()
    start(*z_moves)
    start(to_partner[2])
    rings[0].last()
    recv(to_partner[0])
    rings[2].begin()
    rings[0].done()
    project((0,), own_tokens(0), 0, 0)
    flash(0, 0, 1024, 0, 512)
    flash(0, 0, 1024, 512, 512)
    rings[1].forward()
    start(to_partner[3])
    recv(to_partner[1])
    rings[3].begin()
    recv(*share)
    for h in range(2):
        rows = [wsp[h].reshape(320, 1152)[208:288].astype(jnp.float32)[8:80] for h in range(2)]
        wso[slot] = jnp.concatenate(rows, axis=0).astype(jnp.bfloat16)
    project((1,), own_tokens(0), 0, 0)
    y_rings[0].forward()
    flash(1, 0, 1024, 0, 512)
    flash(1, 0, 1024, 512, 512)
    rings[1].last()
    rings[2].forward()
    recv(z_moves[0])
    y_rings[3].begin()
    rings[1].done()
    project((0, 1), own_tokens(1), 1024, 1024)
    y_rings[0].last()
    rings[2].last()
    for h in range(2):
        flash(h, 1024, 1024, 0, 512)
        flash(h, 1024, 1024, 512, 512)
    recv(to_partner[2])
    rings[4].begin()
    rings[3].forward()
    y_rings[3].forward()
    recv(z_moves[1])
    y_rings[1].begin()
    for h in range(2):
        flash(h, 0, 2048, 1024, 512)
    recv(to_partner[3])
    rings[5].begin()
    rings[3].last()
    y_rings[3].last()
    for h in range(2):
        flash(h, 0, 2048, 1536, 512)
    rings[4].forward()
    y_rings[1].forward()
    recv(z_moves[2])
    y_rings[2].begin()
    rings[2].done()
    project((0, 1), far_tokens(0), None, 2048)
    rings[5].forward()
    wso_ring.begin()
    rings[4].last()
    for h in range(2):
        flash(h, 0, 2048, 2048, 512)
    y_rings[1].last()
    rings[5].last()
    rings[3].done()
    project((0, 1), far_tokens(1), None, 2560)
    wso_ring.forward()
    for h in range(2):
        flash(h, 0, 2048, 2560, 512)
    y_rings[2].forward()
    rings[4].done()
    project((0, 1), far_tokens(2), None, 3072)
    wso_ring.last()
    for h in range(2):
        flash(h, 0, 2048, 3072, 512)
    y_rings[2].last()
    rings[5].done()
    project((0, 1), far_tokens(3), None, 3584)
    for h in range(2):
        flash(h, 0, 2048, 3584, 512)

    for s in range(8):
        for h in range(2):
            for n in range(2):
                part = acc[h, :, pl.ds(n * 1024 + s * 128, 128)]
                heads_t[pl.ds(h * 72, 72), pl.ds(n * 128, 128)] = part[0:72] * (1.0 / part[72:73])
        o_send[s] = heads_t[0:144, :].astype(jnp.bfloat16)
    o_moves = []
    for d in range(1, 8):
        to = turn(x, d // 2, 4) * 2 + turn(c, d % 2, 2)
        frm = turn(x, -(d // 2), 4) * 2 + turn(c, d % 2, 2)
        o_moves.append(
            Move(o_send.at[to], o_recv.at[slot], device(x_=to // 2, c_=lax.rem(to, 2)), o_recv.at[frm])
        )
    start(*o_moves)
    o_recv[slot] = o_send[slot]
    wso_ring.done()
    recv(*o_moves)
    update = dot(o_recv[...].reshape(1152, 256), wso[...].reshape(1152, 1152), 0, 0)
    after = (hid_ref[...].astype(jnp.float32) + mod_s_ref[2:3, :] * update).astype(jnp.bfloat16)
    t_send[...] = after.reshape(16, 16, 1152)

    there = []
    for d in range(1, 16):
        to, frm = turn(frame, d, 16), turn(frame, -d, 16)
        there.append(Move(t_send.at[to], t_recv.at[frame], (to, patch), t_recv.at[frm]))
    start(*there)
    t_recv[frame] = t_send[frame]
    for dz in (0, 3, 1, 2):
        y_rings[dz].done()
    for pair in range(8):
        rows = [wt[2 * pair + k].reshape(288, 1152)[208:288].astype(jnp.float32)[8:80] for k in range(2)]
        wto[pair] = jnp.concatenate(rows, axis=0).astype(jnp.bfloat16)
    recv(*there)
    tokens = t_recv[...].reshape(256, 1152)
    t_moved = modulate(tokens, mod_t_ref)
    key = lax.rem(lax.broadcasted_iota(jnp.int32, (256, 256), 0), 16)
    query = lax.rem(lax.broadcasted_iota(jnp.int32, (256, 256), 1), 16)
    same = key == query
    for h in range(HEADS):
        qkv = dot(wt[h].reshape(288, 1152)[0:224], t_moved, 1, 1)
        q = (qkv[0:72] * Q_SCALE).astype(jnp.bfloat16)
        k = qkv[72:144].astype(jnp.bfloat16)
        v = qkv[144:216].astype(jnp.bfloat16)
        s = jnp.where(same, dot(k, q, 0, 0), LOW)
        p = jnp.exp2(s - jnp.max(s, axis=0, keepdims=True))
        p = (p * (1.0 / jnp.sum(p, axis=0, keepdims=True))).astype(jnp.bfloat16)
        heads_t[pl.ds(h * 72, 72), :] = dot(v, p, 1, 0)
    update = dot(heads_t[...].astype(jnp.bfloat16), wto[...].reshape(1152, 1152), 0, 0)
    block = tokens.astype(jnp.float32) + mod_t_ref[2:3, :] * update
    r_send[...] = block.astype(jnp.bfloat16).reshape(16, 16, 1152)
    back = []
    for d in range(1, 16):
        to, frm = turn(frame, d, 16), turn(frame, -d, 16)
        back.append(Move(r_send.at[to], out_ref.at[frame], (to, patch), out_ref.at[frm]))
    start(*back)
    out_ref[frame] = r_send[frame]
    recv(*back)

    for m in sends:
        if m is cross_near or m is cross_far:
            pl.when(edge)(m.wait_send)
        else:
            m.wait_send()
    assert count[0] <= N_COPIES


def shards(hidden, mod_s, w_s_qkv, w_s_out, mod_t, w_t_qkv, w_t_out):
    w_s = jnp.concatenate([w_s_qkv.T, w_s_out, jnp.zeros((32, 1152), jnp.bfloat16)], axis=0)
    w_t = jnp.concatenate([w_t_qkv.T, w_t_out], axis=0)
    vmem = pl.BlockSpec(memory_space=pltpu.VMEM)
    bf, f32 = jnp.bfloat16, jnp.float32
    out = pl.pallas_call(
        kernel,
        out_shape=jax.ShapeDtypeStruct((16, 16, 1152), bf),
        in_specs=[vmem] * 5,
        out_specs=vmem,
        scratch_shapes=[
            pltpu.VMEM((2, 8, 128, 1152), bf),
            pltpu.VMEM((4, 8, 64, 1152), bf),
            pltpu.VMEM((2, 4, 80, 1152), bf),
            pltpu.VMEM((8, 144, 1152), bf),
            pltpu.VMEM((16, 2, 144, 1152), bf),
            pltpu.VMEM((8, 144, 1152), bf),
            pltpu.VMEM((2, 80, 2048), bf),
            pltpu.VMEM((2, 4096, 80), bf),
            pltpu.VMEM((2, 80, 4096), bf),
            pltpu.VMEM((2, 80, 2048), f32),
            pltpu.VMEM((2, 8, 2048), f32),
            pltpu.VMEM((8, 144, 256), bf),
            pltpu.VMEM((8, 144, 256), bf),
            pltpu.VMEM((16, 16, 1152), bf),
            pltpu.VMEM((16, 16, 1152), bf),
            pltpu.VMEM((16, 16, 1152), bf),
            pltpu.VMEM((1152, 256), f32),
            pltpu.SemaphoreType.DMA((N_COPIES,)),
            pltpu.SemaphoreType.DMA((N_COPIES,)),
        ],
        compiler_params=pltpu.CompilerParams(
            collective_id=0, has_side_effects=True, vmem_limit_bytes=62 * 2**20
        ),
        name="st_block",
    )(hidden.reshape(256, 1152), mod_s, mod_t, w_s, w_t)
    return out.reshape(1, 256, 1152)


def solution(mesh):
    in_specs = (
        P("frame", "patch", None),
        P(),
        P(None, "patch"),
        P("patch", None),
        P(),
        P(None, "frame"),
        P("frame", None),
    )
    out_specs = P("frame", "patch", None)
    return jax.shard_map(shards, mesh=mesh, in_specs=in_specs, out_specs=out_specs, check_vma=False)
```

```python
import functools
import math

import jax
import jax.numpy as jnp
from jax import lax
from jax.experimental import pallas as pl
from jax.experimental.pallas import tpu as pltpu
from jax.sharding import PartitionSpec as P

HEADS = 16
HEAD_DIM = 72
EPS = 1e-06
MESH = pl.DeviceIdType.MESH
Q_SCALE = math.log2(math.e) / math.sqrt(HEAD_DIM)
LOW = -1e30
N_SEND = 16
N_RECV = 72
Y_ORDER = (0, 3, 1, 2)
SCHEDULE = (
    ("C",), ("S", 0), ("M", 0), ("M", 1), ("Y",), ("F", 0), ("S", 1), ("YF", 0),
    ("CS",), ("Z", 0), ("L", 0), ("YL", 0), ("YS", 0), ("Z", 1), ("YS", 1), ("F", 1),
    ("ZS", 0), ("Z", 2), ("L", 1), ("CD",), ("T", 0), ("T", 1), ("F", 2), ("A", 0, 1024, 0),
    ("ZS", 1), ("Z", 3), ("M", 2), ("A", 0, 1024, 512), ("L", 2), ("A", 1024, 1024, 0), ("T", 2), ("F", 3),
    ("A", 1024, 1024, 512), ("ZS", 2), ("YF", 1), ("YF", 2), ("OS",), ("A", 0, 2048, 1024), ("L", 3), ("A", 0, 2048, 1536),
    ("ZS", 3), ("T", 3), ("F", 4), ("A", 0, 2048, 2048), ("YS", 2), ("YL", 1), ("YL", 2), ("A", 0, 2048, 2560),
    ("L", 4), ("T", 4), ("F", 5), ("OF",), ("A", 0, 2048, 3072), ("YF", 3), ("L", 5), ("T", 5),
    ("OL",), ("A", 0, 2048, 3584),
)
TAIL = (
    ("YL", 3),
)


def dot(a, b, ca, cb):
    return lax.dot_general(a, b, (((ca,), (cb,)), ((), ())), preferred_element_type=jnp.float32)


def modulate(tokens, mod_ref):
    values = tokens.astype(jnp.float32)
    mean = jnp.mean(values, axis=-1, keepdims=True)
    centred = values - mean
    var = jnp.mean(centred * centred, axis=-1, keepdims=True)
    normed = centred * lax.rsqrt(var + EPS)
    return (normed * (1.0 + mod_ref[1:2, :]) + mod_ref[0:1, :]).astype(jnp.bfloat16)


def kernel(
    hid_ref, mod_s_ref, mod_t_ref, ws_qkv_ref, ws_out_ref, wt_qkv_ref, wt_out_ref, out_ref,
    tok_a, tok_b, wsp, wso, wt, wto, q_buf, k_buf, v_buf, acc, top, o_send, o_recv,
    t_send, t_recv, r_send, heads_t, moved_t, send_sem, recv_sem,
):
    frame = lax.axis_index("frame")
    patch = lax.axis_index("patch")
    zlo, y = frame // 4, lax.rem(frame, 4)
    zhi, x, c = patch // 8, lax.rem(patch // 2, 4), lax.rem(patch, 2)
    z = zhi * 4 + zlo
    slot = x * 2 + c

    def device(z_=z, y_=y, x_=x, c_=c):
        return (lax.rem(z_, 4) * 4 + y_, (z_ // 4) * 8 + x_ * 2 + c_)

    def turn(value, step, size):
        return lax.rem(value + step + size, size)

    right, left = device(x_=turn(x, 1, 4)), device(x_=turn(x, -1, 4))
    sibling = device(c_=1 - c)
    partner = device(z_=turn(z, 4, 8))
    x_slots = [turn(x, d, 4) * 2 + c for d in range(4)]
    sib_slots = [turn(x, d, 4) * 2 + 1 - c for d in range(4)]

    barrier = pltpu.get_barrier_semaphore()
    greet = [device(x_=turn(x, d // 2, 4), c_=turn(c, d % 2, 2)) for d in range(1, 8)]
    greet += [(turn(frame, d, 16), patch) for d in range(1, 16)]
    greet += [device(z_=turn(z, d, 8)) for d in (4, 1, -1, 2, -2)]
    for other in greet:
        pl.semaphore_signal(barrier, inc=1, device_id=other, device_id_type=MESH)

    send_ids, recv_ids, fresh = {}, {}, [0]

    class Move:
        def __init__(self, src, dst, target, landing, group, recv_group=None):
            self.s = send_ids.setdefault(group, len(send_ids))
            if recv_group is None:
                fresh[0] += 1
                recv_group = fresh[0]
            self.r = recv_ids.setdefault(recv_group, len(recv_ids))
            self.src, self.dst, self.target, self.landing = src, dst, target, landing

        def start(self):
            pltpu.make_async_remote_copy(
                src_ref=self.src, dst_ref=self.dst, send_sem=send_sem.at[self.s],
                recv_sem=recv_sem.at[self.r], device_id=self.target, device_id_type=MESH,
            ).start()

        def wait_recv(self, landing=None):
            landing = self.landing if landing is None else landing
            pltpu.make_async_remote_copy(
                src_ref=landing, dst_ref=landing, send_sem=send_sem.at[self.s],
                recv_sem=recv_sem.at[self.r], device_id=self.target, device_id_type=MESH,
            ).wait_recv()

    def sent(group, ref):
        i = send_ids[group]
        pltpu.make_async_remote_copy(
            src_ref=ref, dst_ref=ref, send_sem=send_sem.at[i],
            recv_sem=recv_sem.at[0], device_id=sibling, device_id_type=MESH,
        ).wait_send()

    def start(*moves):
        for m in moves:
            m.start()

    def recv(*moves):
        for m in moves:
            m.wait_recv()

    class Ring:
        def __init__(self, buf, rows, cut, group, name):
            me, near, far, back = [buf.at[s] for s in x_slots]
            self.buf = buf
            self.to_right = Move(me, me, right, back, group)
            self.to_left = Move(me, me, left, near, group)
            top_half, low_half = pl.ds(0, cut), pl.ds(cut, rows - cut)
            self.on_right = Move(back.at[top_half], back.at[top_half], right, far.at[top_half], group)
            self.on_left = Move(near.at[low_half], near.at[low_half], left, far.at[low_half], group)
            self.sib = [
                Move(buf.at[x_slots[d]], buf.at[x_slots[d]], sibling, None, group, ("sib", name)) for d in range(4)
            ]

        def begin(self):
            start(self.to_right, self.to_left, self.sib[0])

        def forward(self):
            recv(self.to_right)
            start(self.on_right)
            recv(self.to_left)
            start(self.on_left, self.sib[3], self.sib[1])

        def last(self):
            recv(self.on_right, self.on_left)
            start(self.sib[2])

        def done(self):
            self.sib[0].wait_recv(self.buf.at[0:4])

    rings = [Ring(tok_a.at[n], 128, 64, "near", n) for n in range(2)]
    rings += [Ring(tok_b.at[n], 64, 32, "far", n + 2) for n in range(4)]
    to_partner = [
        Move(tok_a.at[n // 2, slot, pl.ds((n % 2) * 64, 64)], tok_b.at[n, slot], partner, tok_b.at[n, slot], "z")
        for n in range(4)
    ]
    wso_ring = Ring(wso, 144, 64, "wso", 6)

    edge = jnp.logical_or(zlo == 0, zlo == 3)
    ahead = jnp.where(zlo == 0, -1, 1)
    cross_src = wsp.at[0, y]
    cross_dst = wsp.at[1, y]
    cross_near = Move(cross_src, cross_dst, device(z_=turn(z, ahead, 8)), cross_dst, "c1", "cross")
    cross_far = Move(cross_src, cross_dst, device(z_=turn(z, 2 * ahead, 8)), cross_dst, "c2", "cross")
    share = [Move(cross_dst, cross_dst, device(y_=turn(y, d, 4)), None, "share", "share") for d in (1, 3, 2)]

    def wt_slot(dz, dy):
        return turn(zlo, dz, 4) * 4 + turn(y, dy, 4)

    def wt_half(dz, dy):
        return wt.at[wt_slot(dz, dy), c]

    two = jnp.where(c == 0, 2, -2)
    z_moves = [
        Move(wt_half(0, 0), wt_half(0, 0), device(z_=turn(z, 1, 8)), wt_half(-1, 0), "zw"),
        Move(wt_half(0, 0), wt_half(0, 0), device(z_=turn(z, -1, 8)), wt_half(1, 0), "zw"),
        Move(wt_half(0, 0), wt_half(0, 0), device(z_=turn(z, two, 8)), wt_half(2, 0), "zw"),
    ]
    y_up, y_down = device(y_=turn(y, 1, 4)), device(y_=turn(y, -1, 4))

    class YRing:
        def __init__(self, dz):
            me, near, far, back = [wt_half(dz, d) for d in range(4)]
            self.up = Move(me, me, y_up, back, "y")
            self.down = Move(me, me, y_down, near, "y")
            first, second = pl.ds(0, 64), pl.ds(64, 80)
            self.on_up = Move(back.at[first], back.at[first], y_up, far.at[first], "y")
            self.on_down = Move(near.at[second], near.at[second], y_down, far.at[second], "y")
            self.sib = [
                Move(wt_half(dz, d), wt_half(dz, d), sibling, None, "ysib", "ysib")
                for d in range(4) if (dz, d) != (0, 0)
            ]

        def begin(self):
            start(self.up, self.down)
            if len(self.sib) == 4:
                start(self.sib[0])

        def forward(self):
            recv(self.up)
            start(self.on_up)
            recv(self.down)
            start(self.on_down, self.sib[-1], self.sib[-3])

        def last(self):
            recv(self.on_up, self.on_down)
            start(self.sib[-2])

    y_rings = {dz: YRing(dz) for dz in Y_ORDER}

    def project(heads, ref, q_at, k_at):
        tokens = ref[...].reshape(-1, 1152)
        n = tokens.shape[0]
        for h in heads:
            qkv = dot(wsp[h].reshape(320, 1152)[0:224], tokens, 1, 1)
            if q_at is not None:
                q = jnp.concatenate([qkv[0:72] * Q_SCALE, jnp.zeros((8, n), jnp.float32)], axis=0)
                q_buf[h, :, pl.ds(q_at, n)] = q.astype(jnp.bfloat16)
            k = jnp.concatenate([qkv[72:144], jnp.zeros((8, n), jnp.float32)], axis=0)
            k_buf[h, pl.ds(k_at, n), :] = k.T.astype(jnp.bfloat16)
            row = lax.broadcasted_iota(jnp.int32, (8, n), 0)
            one = jnp.where(row == 0, 1.0, 0.0)
            v_buf[h, :, pl.ds(k_at, n)] = jnp.concatenate([qkv[144:216], one], axis=0).astype(jnp.bfloat16)

    def flash(h, q_at, q_n, k_at, k_n):
        qs, ks = pl.ds(q_at, q_n), pl.ds(k_at, k_n)
        s = dot(k_buf[h, ks, :], q_buf[h, :, qs], 1, 0)
        before = top[h, 0:1, qs]
        now = jnp.maximum(before, jnp.max(s, axis=0, keepdims=True))
        p = jnp.exp2(s - now).astype(jnp.bfloat16)
        acc[h, :, qs] = acc[h, :, qs] * jnp.exp2(before - now) + dot(v_buf[h, :, ks], p, 1, 0)
        top[h, 0:1, qs] = now

    moved = modulate(hid_ref[...], mod_s_ref)
    tok_a[0, slot] = moved[0:128]
    tok_a[1, slot] = moved[128:256]
    f32 = jnp.float32
    own = [ws_qkv_ref[...].astype(f32), ws_out_ref[...].astype(f32), jnp.zeros((32, 1152), f32)]
    wsp[0] = jnp.concatenate(own, axis=0).astype(jnp.bfloat16).reshape(4, 80, 1152)
    own = [wt_qkv_ref[...].astype(f32), wt_out_ref[...].astype(f32)]
    wt[frame] = jnp.concatenate(own, axis=0).astype(jnp.bfloat16).reshape(2, 144, 1152)
    acc[...] = jnp.zeros_like(acc)
    top[...] = jnp.full_like(top, LOW)
    pl.semaphore_wait(barrier, len(greet))

    def cross_start():
        @pl.when(edge)
        def _():
            cross_near.start()
            cross_far.start()

    def cross_share():
        recv(cross_near)
        start(*share)

    def share_done():
        share[0].wait_recv(wsp.at[1, 0:3])
        rows = [wsp[h].reshape(320, 1152)[208:288].astype(jnp.float32)[8:80] for h in range(2)]
        wso[slot] = jnp.concatenate(rows, axis=0).astype(jnp.bfloat16)

    def forward_z(n):
        recv(to_partner[n])
        rings[n + 2].begin()

    def forward_y(i):
        recv(z_moves[i])
        y_rings[Y_ORDER[i + 1]].begin()

    def tokens_done(n):
        rings[n].done()
        project((0, 1), *chunks[n])

    def attend(q_at, q_n, k_at):
        for h in range(2):
            flash(h, q_at, q_n, k_at, 512)

    chunks = [(tok_a.at[n], n * 1024, n * 1024) for n in range(2)]
    chunks += [(tok_b.at[n], None, 2048 + n * 512) for n in range(4)]
    steps = {
        "S": lambda n: rings[n].begin(),
        "F": lambda n: rings[n].forward(),
        "L": lambda n: rings[n].last(),
        "T": tokens_done,
        "A": attend,
        "Z": lambda n: to_partner[n].start(),
        "ZS": forward_z,
        "C": cross_start,
        "CS": cross_share,
        "CD": share_done,
        "M": lambda i: z_moves[i].start(),
        "Y": lambda: y_rings[0].begin(),
        "YS": forward_y,
        "YF": lambda i: y_rings[Y_ORDER[i]].forward(),
        "YL": lambda i: y_rings[Y_ORDER[i]].last(),
        "YD": lambda i: y_rings[Y_ORDER[i]].done(),
        "OS": lambda: wso_ring.begin(),
        "OF": lambda: wso_ring.forward(),
        "OL": lambda: wso_ring.last(),
    }
    for step in SCHEDULE:
        steps[step[0]](*step[1:])

    for s in range(8):
        for h in range(2):
            for n in range(2):
                part = acc[h, :, pl.ds(n * 1024 + s * 128, 128)]
                heads_t[pl.ds(h * 72, 72), pl.ds(n * 128, 128)] = part[0:72] * (1.0 / part[72:73])
        o_send[s] = heads_t[0:144, :].astype(jnp.bfloat16)
    o_moves = []
    for d in range(1, 8):
        to = turn(x, d // 2, 4) * 2 + turn(c, d % 2, 2)
        o_moves.append(
            Move(o_send.at[to], o_recv.at[slot], device(x_=to // 2, c_=lax.rem(to, 2)), None, "o", "o")
        )
    start(*o_moves)
    o_recv[slot] = o_send[slot]
    for step in TAIL:
        steps[step[0]](*step[1:])
    wso_ring.done()
    o_moves[0].wait_recv(o_recv.at[0:7])
    update = dot(o_recv[...].reshape(1152, 256), wso[...].reshape(1152, 1152), 0, 0)
    after = (hid_ref[...].astype(jnp.float32) + mod_s_ref[2:3, :] * update).astype(jnp.bfloat16)
    t_send[...] = after.reshape(16, 16, 1152)

    there = []
    for d in range(1, 16):
        to = turn(frame, d, 16)
        there.append(Move(t_send.at[to], t_recv.at[frame], (to, patch), None, "there", "there"))
    start(*there)
    t_recv[frame] = t_send[frame]
    y_rings[0].sib[0].wait_recv(wt.at[0:15, 0])
    for pair in range(8):
        rows = [wt[2 * pair + k].reshape(288, 1152)[208:288].astype(jnp.float32)[8:80] for k in range(2)]
        wto[pair] = jnp.concatenate(rows, axis=0).astype(jnp.bfloat16)
    there[0].wait_recv(t_recv.at[0:15])
    tokens = t_recv[...].reshape(256, 1152)
    t_moved = modulate(tokens, mod_t_ref)
    key = lax.rem(lax.broadcasted_iota(jnp.int32, (256, 256), 0), 16)
    query = lax.rem(lax.broadcasted_iota(jnp.int32, (256, 256), 1), 16)
    bias = jnp.where(key == query, 0.0, LOW)
    one = jnp.where(lax.broadcasted_iota(jnp.int32, (8, 256), 0) == 0, 1.0, 0.0)
    moved_t[...] = t_moved.astype(f32).T.astype(jnp.bfloat16)

    def four_heads(g, _):
        qkv = dot(wt[pl.ds(4 * g, 4)].reshape(1152, 1152), moved_t[...], 1, 0)
        for i in range(4):
            part = qkv[288 * i:288 * i + 216]
            q = (part[0:72] * Q_SCALE).astype(jnp.bfloat16)
            k = part[72:144].T.astype(jnp.bfloat16)
            v = jnp.concatenate([part[144:216], one], axis=0).astype(jnp.bfloat16)
            s = dot(k, q, 1, 0) + bias
            p = jnp.exp2(s - jnp.max(s, axis=0, keepdims=True)).astype(jnp.bfloat16)
            o = dot(v, p, 1, 0)
            rows = pl.ds(pl.multiple_of((4 * g + i) * 72, 8), 72)
            heads_t[rows, :] = o[0:72] * (1.0 / o[72:73])
        return 0

    lax.fori_loop(0, 4, four_heads, 0)
    update = dot(heads_t[...].astype(jnp.bfloat16), wto[...].reshape(1152, 1152), 0, 0)
    block = tokens.astype(jnp.float32) + mod_t_ref[2:3, :] * update
    r_send[...] = block.astype(jnp.bfloat16).reshape(16, 16, 1152)
    back = []
    for d in range(1, 16):
        to = turn(frame, d, 16)
        back.append(Move(r_send.at[to], out_ref.at[frame], (to, patch), None, "back", "back"))
    start(*back)
    out_ref[frame] = r_send[frame]
    back[0].wait_recv(out_ref.at[0:15])

    sent("near", tok_b.at[0:4, 0:7])
    sent("far", tok_b.at[0:4, 0:7])
    sent("wso", wso.at[0:7])
    sent("z", tok_b.at[0, 0:4])
    sent("share", wsp.at[1, 0:3])
    sent("zw", wso.at[0:3])
    sent("y", wt.at[0:6])
    sent("ysib", wt.at[0:15, 0])
    sent("o", o_recv.at[0:7])
    sent("there", t_recv.at[0:15])
    sent("back", t_recv.at[0:15])

    @pl.when(edge)
    def _():
        sent("c1", cross_src)
        sent("c2", cross_src)

    assert len(send_ids) <= N_SEND and len(recv_ids) <= N_RECV


def shards(hidden, mod_s, w_s_qkv, w_s_out, mod_t, w_t_qkv, w_t_out):
    vmem = pl.BlockSpec(memory_space=pltpu.VMEM)
    bf, f32 = jnp.bfloat16, jnp.float32
    out = pl.pallas_call(
        kernel,
        out_shape=jax.ShapeDtypeStruct((16, 16, 1152), bf),
        in_specs=[vmem] * 7,
        out_specs=vmem,
        scratch_shapes=[
            pltpu.VMEM((2, 8, 128, 1152), bf),
            pltpu.VMEM((4, 8, 64, 1152), bf),
            pltpu.VMEM((2, 4, 80, 1152), bf),
            pltpu.VMEM((8, 144, 1152), bf),
            pltpu.VMEM((16, 2, 144, 1152), bf),
            pltpu.VMEM((8, 144, 1152), bf),
            pltpu.VMEM((2, 80, 2048), bf),
            pltpu.VMEM((2, 4096, 80), bf),
            pltpu.VMEM((2, 80, 4096), bf),
            pltpu.VMEM((2, 80, 2048), f32),
            pltpu.VMEM((2, 8, 2048), f32),
            pltpu.VMEM((8, 144, 256), bf),
            pltpu.VMEM((8, 144, 256), bf),
            pltpu.VMEM((16, 16, 1152), bf),
            pltpu.VMEM((16, 16, 1152), bf),
            pltpu.VMEM((16, 16, 1152), bf),
            pltpu.VMEM((1152, 256), f32),
            pltpu.VMEM((1152, 256), bf),
            pltpu.SemaphoreType.DMA((N_SEND,)),
            pltpu.SemaphoreType.DMA((N_RECV,)),
        ],
        compiler_params=pltpu.CompilerParams(
            collective_id=0, has_side_effects=True, vmem_limit_bytes=62 * 2**20
        ),
        name="st_block",
    )(hidden.reshape(256, 1152), mod_s, mod_t, w_s_qkv.T, w_s_out, w_t_qkv.T, w_t_out)
    return out.reshape(1, 256, 1152)


def solution(mesh):
    in_specs = (
        P("frame", "patch", None),
        P(),
        P(None, "patch"),
        P("patch", None),
        P(),
        P(None, "frame"),
        P("frame", None),
    )
    out_specs = P("frame", "patch", None)
    return jax.shard_map(shards, mesh=mesh, in_specs=in_specs, out_specs=out_specs, check_vma=False)
```

```python
import functools
import math

import jax
import jax.numpy as jnp
from jax import lax
from jax.experimental import pallas as pl
from jax.experimental.pallas import tpu as pltpu
from jax.sharding import PartitionSpec as P

HEADS = 16
HEAD_DIM = 72
EPS = 1e-06
MESH = pl.DeviceIdType.MESH
Q_SCALE = math.log2(math.e) / math.sqrt(HEAD_DIM)
LOW = -1e30
N_SEND = 16
N_RECV = 72
Y_ORDER = (0, 3, 1, 2)
SCHEDULE = (
    ("S", 0), ("Z", 1), ("C",), ("S", 1), ("F", 0), ("F", 1), ("Z", 2), ("CS",),
    ("L", 0), ("L", 1), ("ZS", 1), ("T", 0), ("Z", 0), ("T", 1), ("CD",), ("U", 0),
    ("ZS", 2), ("A", 0, 1024, 0), ("U", 1), ("OS",), ("A", 0, 1024, 512), ("Z", 3), ("F", 3), ("Y",),
    ("A", 1024, 1024, 512), ("A", 0, 2048, 1024), ("ZS", 0), ("M", 0), ("A", 0, 2048, 1536), ("L", 3), ("F", 4), ("A", 1024, 1024, 0),
    ("M", 1), ("F", 2), ("T", 3), ("YF", 0), ("U", 3), ("ZS", 3), ("L", 4), ("A", 0, 2048, 2560),
    ("T", 4), ("M", 2), ("L", 2), ("U", 4), ("YS", 0), ("F", 5), ("A", 0, 2048, 3072), ("T", 2),
    ("L", 5), ("OF",), ("YS", 1), ("U", 2), ("A", 0, 2048, 2048), ("T", 5), ("U", 5), ("YS", 2),
    ("YF", 1),
)
TAIL = (
    ("OL",),
)
LAST_KEYS = 3584
LATE = (
    ("YL", 1), ("YF", 2), ("YL", 0), ("YF", 3), ("YL", 2), ("YL", 3),
)


def dot(a, b, ca, cb):
    return lax.dot_general(a, b, (((ca,), (cb,)), ((), ())), preferred_element_type=jnp.float32)


def modulate(tokens, mod_ref):
    values = tokens.astype(jnp.float32)
    mean = jnp.mean(values, axis=-1, keepdims=True)
    centred = values - mean
    var = jnp.mean(centred * centred, axis=-1, keepdims=True)
    normed = centred * lax.rsqrt(var + EPS)
    return (normed * (1.0 + mod_ref[1:2, :]) + mod_ref[0:1, :]).astype(jnp.bfloat16)


def kernel(
    hid_ref, mod_s_ref, mod_t_ref, ws_qkv_ref, ws_out_ref, wt_qkv_ref, wt_out_ref, out_ref,
    tok_a, tok_b, wsp, wso, wt, wto, q_buf, k_buf, v_buf, acc, top, o_send, o_recv,
    t_send, t_recv, r_send, heads_t, moved_t, send_sem, recv_sem,
):
    frame = lax.axis_index("frame")
    patch = lax.axis_index("patch")
    zlo, y = frame // 4, lax.rem(frame, 4)
    zhi, x, c = patch // 8, lax.rem(patch // 2, 4), lax.rem(patch, 2)
    z = zhi * 4 + zlo
    slot = x * 2 + c

    def device(z_=z, y_=y, x_=x, c_=c):
        return (lax.rem(z_, 4) * 4 + y_, (z_ // 4) * 8 + x_ * 2 + c_)

    def turn(value, step, size):
        return lax.rem(value + step + size, size)

    right, left = device(x_=turn(x, 1, 4)), device(x_=turn(x, -1, 4))
    sibling = device(c_=1 - c)
    partner = device(z_=turn(z, 4, 8))
    x_slots = [turn(x, d, 4) * 2 + c for d in range(4)]
    sib_slots = [turn(x, d, 4) * 2 + 1 - c for d in range(4)]

    barrier = pltpu.get_barrier_semaphore()
    greet = [device(x_=turn(x, d // 2, 4), c_=turn(c, d % 2, 2)) for d in range(1, 8)]
    greet += [(turn(frame, d, 16), patch) for d in range(1, 16)]
    greet += [device(z_=turn(z, d, 8)) for d in (4, 1, -1, 2, -2)]
    for other in greet:
        pl.semaphore_signal(barrier, inc=1, device_id=other, device_id_type=MESH)

    send_ids, recv_ids, fresh = {}, {}, [0]

    class Move:
        def __init__(self, src, dst, target, landing, group, recv_group=None):
            self.s = send_ids.setdefault(group, len(send_ids))
            if recv_group is None:
                fresh[0] += 1
                recv_group = fresh[0]
            self.r = recv_ids.setdefault(recv_group, len(recv_ids))
            self.src, self.dst, self.target, self.landing = src, dst, target, landing

        def start(self):
            pltpu.make_async_remote_copy(
                src_ref=self.src, dst_ref=self.dst, send_sem=send_sem.at[self.s],
                recv_sem=recv_sem.at[self.r], device_id=self.target, device_id_type=MESH,
            ).start()

        def wait_recv(self, landing=None):
            landing = self.landing if landing is None else landing
            pltpu.make_async_remote_copy(
                src_ref=landing, dst_ref=landing, send_sem=send_sem.at[self.s],
                recv_sem=recv_sem.at[self.r], device_id=self.target, device_id_type=MESH,
            ).wait_recv()

    def sent(group, ref):
        i = send_ids[group]
        pltpu.make_async_remote_copy(
            src_ref=ref, dst_ref=ref, send_sem=send_sem.at[i],
            recv_sem=recv_sem.at[0], device_id=sibling, device_id_type=MESH,
        ).wait_send()

    def start(*moves):
        for m in moves:
            m.start()

    def recv(*moves):
        for m in moves:
            m.wait_recv()

    class Ring:
        def __init__(self, buf, rows, cut, group, name):
            me, near, far, back = [buf.at[s] for s in x_slots]
            self.buf = buf
            self.to_right = Move(me, me, right, back, group)
            self.to_left = Move(me, me, left, near, group)
            top_half, low_half = pl.ds(0, cut), pl.ds(cut, rows - cut)
            self.on_right = Move(back.at[top_half], back.at[top_half], right, far.at[top_half], group)
            self.on_left = Move(near.at[low_half], near.at[low_half], left, far.at[low_half], group)
            self.sib = [
                Move(buf.at[x_slots[d]], buf.at[x_slots[d]], sibling, None, group, ("sib", name)) for d in range(4)
            ]

        def begin(self):
            start(self.to_right, self.to_left, self.sib[0])

        def forward(self):
            recv(self.to_right)
            start(self.on_right)
            recv(self.to_left)
            start(self.on_left, self.sib[3], self.sib[1])

        def last(self):
            recv(self.on_right, self.on_left)
            start(self.sib[2])

        def done(self):
            self.sib[0].wait_recv(self.buf.at[0:4])

    rings = [Ring(tok_a.at[n], 128, 64, "near", n) for n in range(2)]
    rings += [Ring(tok_b.at[n], 64, 32, "far", n + 2) for n in range(4)]
    to_partner = [
        Move(tok_a.at[n // 2, slot, pl.ds((n % 2) * 64, 64)], tok_b.at[n, slot], partner, tok_b.at[n, slot], "z")
        for n in range(4)
    ]
    wso_ring = Ring(wso, 144, 64, "wso", 6)

    edge = jnp.logical_or(zlo == 0, zlo == 3)
    ahead = jnp.where(zlo == 0, -1, 1)
    cross_src = wsp.at[0, y]
    cross_dst = wsp.at[1, y]
    cross_near = Move(cross_src, cross_dst, device(z_=turn(z, ahead, 8)), cross_dst, "c1", "cross")
    cross_far = Move(cross_src, cross_dst, device(z_=turn(z, 2 * ahead, 8)), cross_dst, "c2", "cross")
    share = [Move(cross_dst, cross_dst, device(y_=turn(y, d, 4)), None, "share", "share") for d in (1, 3, 2)]

    def wt_slot(dz, dy):
        return turn(zlo, dz, 4) * 4 + turn(y, dy, 4)

    def wt_half(dz, dy):
        return wt.at[wt_slot(dz, dy), c]

    two = jnp.where(c == 0, 2, -2)
    z_moves = [
        Move(wt_half(0, 0), wt_half(0, 0), device(z_=turn(z, 1, 8)), wt_half(-1, 0), "zw"),
        Move(wt_half(0, 0), wt_half(0, 0), device(z_=turn(z, -1, 8)), wt_half(1, 0), "zw"),
        Move(wt_half(0, 0), wt_half(0, 0), device(z_=turn(z, two, 8)), wt_half(2, 0), "zw"),
    ]
    y_up, y_down = device(y_=turn(y, 1, 4)), device(y_=turn(y, -1, 4))

    class YRing:
        def __init__(self, dz):
            me, near, far, back = [wt_half(dz, d) for d in range(4)]
            self.up = Move(me, me, y_up, back, "y")
            self.down = Move(me, me, y_down, near, "y")
            first, second = pl.ds(0, 64), pl.ds(64, 80)
            self.on_up = Move(back.at[first], back.at[first], y_up, far.at[first], "y")
            self.on_down = Move(near.at[second], near.at[second], y_down, far.at[second], "y")
            self.sib = [
                Move(wt_half(dz, d), wt_half(dz, d), sibling, None, "ysib", "ysib")
                for d in range(4) if (dz, d) != (0, 0)
            ]

        def begin(self):
            start(self.up, self.down)
            if len(self.sib) == 4:
                start(self.sib[0])

        def forward(self):
            recv(self.up)
            start(self.on_up)
            recv(self.down)
            start(self.on_down, self.sib[-1], self.sib[-3])

        def last(self):
            recv(self.on_up, self.on_down)
            start(self.sib[-2])

    y_rings = {dz: YRing(dz) for dz in Y_ORDER}

    def project(heads, ref, q_at, k_at):
        tokens = ref[...].reshape(-1, 1152)
        n = tokens.shape[0]
        for h in heads:
            qkv = dot(wsp[h].reshape(320, 1152)[0:224], tokens, 1, 1)
            if q_at is not None:
                q = jnp.concatenate([qkv[0:72] * Q_SCALE, jnp.zeros((8, n), jnp.float32)], axis=0)
                q_buf[h, :, pl.ds(q_at, n)] = q.astype(jnp.bfloat16)
            k = jnp.concatenate([qkv[72:144], jnp.zeros((8, n), jnp.float32)], axis=0)
            k_buf[h, pl.ds(k_at, n), :] = k.T.astype(jnp.bfloat16)
            row = lax.broadcasted_iota(jnp.int32, (8, n), 0)
            one = jnp.where(row == 0, 1.0, 0.0)
            v_buf[h, :, pl.ds(k_at, n)] = jnp.concatenate([qkv[144:216], one], axis=0).astype(jnp.bfloat16)

    def flash(h, q_at, q_n, k_at, k_n):
        qs, ks = pl.ds(q_at, q_n), pl.ds(k_at, k_n)
        s = dot(k_buf[h, ks, :], q_buf[h, :, qs], 1, 0)
        before = top[h, 0:1, qs]
        now = jnp.maximum(before, jnp.max(s, axis=0, keepdims=True))
        p = jnp.exp2(s - now).astype(jnp.bfloat16)
        acc[h, :, qs] = acc[h, :, qs] * jnp.exp2(before - now) + dot(v_buf[h, :, ks], p, 1, 0)
        top[h, 0:1, qs] = now

    moved = modulate(hid_ref[...], mod_s_ref)
    tok_a[0, slot] = moved[0:128]
    tok_a[1, slot] = moved[128:256]
    f32 = jnp.float32
    own = [ws_qkv_ref[...].astype(f32), ws_out_ref[...].astype(f32), jnp.zeros((32, 1152), f32)]
    wsp[0] = jnp.concatenate(own, axis=0).astype(jnp.bfloat16).reshape(4, 80, 1152)
    own = [wt_qkv_ref[...].astype(f32), wt_out_ref[...].astype(f32)]
    wt[frame] = jnp.concatenate(own, axis=0).astype(jnp.bfloat16).reshape(2, 144, 1152)
    acc[...] = jnp.zeros_like(acc)
    top[...] = jnp.full_like(top, LOW)
    pl.semaphore_wait(barrier, len(greet))

    def cross_start():
        @pl.when(edge)
        def _():
            cross_near.start()
            cross_far.start()

    def cross_share():
        recv(cross_near)
        start(*share)

    def share_done():
        share[0].wait_recv(wsp.at[1, 0:3])
        rows = [wsp[h].reshape(320, 1152)[208:288].astype(jnp.float32)[8:80] for h in range(2)]
        wso[slot] = jnp.concatenate(rows, axis=0).astype(jnp.bfloat16)

    def forward_z(n):
        recv(to_partner[n])
        rings[n + 2].begin()

    def forward_y(i):
        recv(z_moves[i])
        y_rings[Y_ORDER[i + 1]].begin()

    def tokens_done(n):
        rings[n].done()
        project((0,), *chunks[n])

    def attend(q_at, q_n, k_at):
        for h in range(2):
            flash(h, q_at, q_n, k_at, 512)

    chunks = [(tok_a.at[n], n * 1024, n * 1024) for n in range(2)]
    chunks += [(tok_b.at[n], None, 2048 + n * 512) for n in range(4)]
    steps = {
        "S": lambda n: rings[n].begin(),
        "F": lambda n: rings[n].forward(),
        "L": lambda n: rings[n].last(),
        "T": tokens_done,
        "U": lambda n: project((1,), *chunks[n]),
        "A": attend,
        "Z": lambda n: to_partner[n].start(),
        "ZS": forward_z,
        "C": cross_start,
        "CS": cross_share,
        "CD": share_done,
        "M": lambda i: z_moves[i].start(),
        "Y": lambda: y_rings[0].begin(),
        "YS": forward_y,
        "YF": lambda i: y_rings[Y_ORDER[i]].forward(),
        "YL": lambda i: y_rings[Y_ORDER[i]].last(),
        "YD": lambda i: y_rings[Y_ORDER[i]].done(),
        "OS": lambda: wso_ring.begin(),
        "OF": lambda: wso_ring.forward(),
        "OL": lambda: wso_ring.last(),
    }
    for step in SCHEDULE:
        steps[step[0]](*step[1:])

    def heads_back(n):
        attend(n * 1024, 1024, LAST_KEYS)
        for s in range(8):
            pair = []
            for h in range(2):
                part = acc[h, :, pl.ds(n * 1024 + s * 128, 128)]
                pair.append(part[0:72] * (1.0 / part[72:73]))
            o_send[n, s] = jnp.concatenate(pair, axis=0).astype(jnp.bfloat16)
        moves = []
        for d in range(1, 8):
            to = turn(x, d // 2, 4) * 2 + turn(c, d % 2, 2)
            target = device(x_=to // 2, c_=lax.rem(to, 2))
            moves.append(Move(o_send.at[n, to], o_recv.at[n, slot], target, None, "o", ("o", n)))
        start(*moves)
        o_recv[n, slot] = o_send[n, slot]
        return moves

    my_rows = y * 4 + zlo

    def spatial_end(n, moves):
        moves[0].wait_recv(o_recv.at[n, 0:7])
        update = dot(o_recv[n].reshape(1152, 128), wso[...].reshape(1152, 1152), 0, 0)
        old = hid_ref[pl.ds(n * 128, 128), :].astype(f32)
        after = (old + mod_s_ref[2:3, :] * update).astype(jnp.bfloat16)
        t_send[pl.ds(8 * n, 8)] = after.reshape(8, 16, 1152)
        moves = []
        for dz in (2, 1, 3, 0):
            for to_y in (2 * n, 2 * n + 1):
                to_z = turn(zlo, dz, 4)
                move = Move(
                    t_send.at[4 * to_y + to_z], t_recv.at[frame], (4 * to_z + to_y, patch), None, "there", "there"
                )
                if dz == 0:
                    pl.when(y != to_y)(move.start)
                else:
                    move.start()
                moves.append(move)
        return moves

    first = heads_back(0)
    second = heads_back(1)
    for step in TAIL:
        steps[step[0]](*step[1:])
    wso_ring.done()
    there = spatial_end(0, first)
    spatial_end(1, second)

    t_recv[frame] = t_send[my_rows]
    for step in LATE:
        steps[step[0]](*step[1:])
    y_rings[0].sib[0].wait_recv(wt.at[0:15, 0])
    for pair in range(8):
        rows = [wt[2 * pair + k].reshape(288, 1152)[208:288].astype(jnp.float32)[8:80] for k in range(2)]
        wto[pair] = jnp.concatenate(rows, axis=0).astype(jnp.bfloat16)
    there[0].wait_recv(t_recv.at[0:15])
    tokens = t_recv[...].reshape(256, 1152)
    t_moved = modulate(tokens, mod_t_ref)
    key = lax.rem(lax.broadcasted_iota(jnp.int32, (256, 256), 0), 16)
    query = lax.rem(lax.broadcasted_iota(jnp.int32, (256, 256), 1), 16)
    bias = jnp.where(key == query, 0.0, LOW)
    one = jnp.where(lax.broadcasted_iota(jnp.int32, (8, 256), 0) == 0, 1.0, 0.0)
    moved_t[...] = t_moved.astype(f32).T.astype(jnp.bfloat16)

    def four_heads(g, _):
        qkv = dot(wt[pl.ds(4 * g, 4)].reshape(1152, 1152), moved_t[...], 1, 0)
        for i in range(4):
            part = qkv[288 * i:288 * i + 216]
            q = (part[0:72] * Q_SCALE).astype(jnp.bfloat16)
            k = part[72:144].T.astype(jnp.bfloat16)
            v = jnp.concatenate([part[144:216], one], axis=0).astype(jnp.bfloat16)
            s = dot(k, q, 1, 0) + bias
            p = jnp.exp2(s - jnp.max(s, axis=0, keepdims=True)).astype(jnp.bfloat16)
            o = dot(v, p, 1, 0)
            rows = pl.ds(pl.multiple_of((4 * g + i) * 72, 8), 72)
            heads_t[rows, :] = o[0:72] * (1.0 / o[72:73])
        return 0

    lax.fori_loop(0, 4, four_heads, 0)
    update = dot(heads_t[...].astype(jnp.bfloat16), wto[...].reshape(1152, 1152), 0, 0)
    block = tokens.astype(jnp.float32) + mod_t_ref[2:3, :] * update
    r_send[...] = block.astype(jnp.bfloat16).reshape(16, 16, 1152)
    back = []
    for d in range(1, 16):
        to = turn(frame, d, 16)
        back.append(Move(r_send.at[to], out_ref.at[my_rows], (to, patch), None, "back", "back"))
    start(*back)
    out_ref[my_rows] = r_send[frame]
    back[0].wait_recv(out_ref.at[0:15])

    sent("near", tok_b.at[0:4, 0:7])
    sent("far", tok_b.at[0:4, 0:7])
    sent("wso", wso.at[0:7])
    sent("z", tok_b.at[0, 0:4])
    sent("share", wsp.at[1, 0:3])
    sent("zw", wso.at[0:3])
    sent("y", wt.at[0:6])
    sent("ysib", wt.at[0:15, 0])
    sent("o", o_recv.at[0:2, 0:7])
    sent("there", t_recv.at[0:15])
    sent("back", t_recv.at[0:15])

    @pl.when(edge)
    def _():
        sent("c1", cross_src)
        sent("c2", cross_src)

    assert len(send_ids) <= N_SEND and len(recv_ids) <= N_RECV


def shards(hidden, mod_s, w_s_qkv, w_s_out, mod_t, w_t_qkv, w_t_out):
    vmem = pl.BlockSpec(memory_space=pltpu.VMEM)
    bf, f32 = jnp.bfloat16, jnp.float32
    out = pl.pallas_call(
        kernel,
        out_shape=jax.ShapeDtypeStruct((16, 16, 1152), bf),
        in_specs=[vmem] * 7,
        out_specs=vmem,
        scratch_shapes=[
            pltpu.VMEM((2, 8, 128, 1152), bf),
            pltpu.VMEM((4, 8, 64, 1152), bf),
            pltpu.VMEM((2, 4, 80, 1152), bf),
            pltpu.VMEM((8, 144, 1152), bf),
            pltpu.VMEM((16, 2, 144, 1152), bf),
            pltpu.VMEM((8, 144, 1152), bf),
            pltpu.VMEM((2, 80, 2048), bf),
            pltpu.VMEM((2, 4096, 80), bf),
            pltpu.VMEM((2, 80, 4096), bf),
            pltpu.VMEM((2, 80, 2048), f32),
            pltpu.VMEM((2, 8, 2048), f32),
            pltpu.VMEM((2, 8, 144, 128), bf),
            pltpu.VMEM((2, 8, 144, 128), bf),
            pltpu.VMEM((16, 16, 1152), bf),
            pltpu.VMEM((16, 16, 1152), bf),
            pltpu.VMEM((16, 16, 1152), bf),
            pltpu.VMEM((1152, 256), f32),
            pltpu.VMEM((1152, 256), bf),
            pltpu.SemaphoreType.DMA((N_SEND,)),
            pltpu.SemaphoreType.DMA((N_RECV,)),
        ],
        compiler_params=pltpu.CompilerParams(
            collective_id=0, has_side_effects=True, vmem_limit_bytes=62 * 2**20
        ),
        name="st_block",
    )(hidden.reshape(256, 1152), mod_s, mod_t, w_s_qkv.T, w_s_out, w_t_qkv.T, w_t_out)
    return out.reshape(1, 256, 1152)


def solution(mesh):
    in_specs = (
        P("frame", "patch", None),
        P(),
        P(None, "patch"),
        P("patch", None),
        P(),
        P(None, "frame"),
        P("frame", None),
    )
    out_specs = P("frame", "patch", None)
    return jax.shard_map(shards, mesh=mesh, in_specs=in_specs, out_specs=out_specs, check_vma=False)
```

```python
import functools
import math

import jax
import jax.numpy as jnp
from jax import lax
from jax.experimental import pallas as pl
from jax.experimental.pallas import tpu as pltpu
from jax.sharding import PartitionSpec as P

HEADS = 16
HEAD_DIM = 72
EPS = 1e-06
MESH = pl.DeviceIdType.MESH
Q_SCALE = math.log2(math.e) / math.sqrt(HEAD_DIM)
LOW = -1e30
N_SEND = 16
N_RECV = 72
Y_ORDER = (0, 3, 1, 2)
SCHEDULE = (
    ("S", 0), ("Z", 1), ("C",), ("S", 1), ("F", 0), ("F", 1), ("Z", 2), ("CS",),
    ("L", 0), ("L", 1), ("ZS", 1), ("T", 0), ("Z", 0), ("T", 1), ("CD",), ("U", 0),
    ("ZS", 2), ("A", 0, 1024, 0), ("U", 1), ("OS",), ("A", 0, 1024, 512), ("Z", 3), ("F", 3), ("Y",),
    ("A", 1024, 1024, 512), ("A", 0, 2048, 1024), ("ZS", 0), ("M", 0), ("A", 0, 2048, 1536), ("L", 3), ("F", 4), ("A", 1024, 1024, 0),
    ("M", 1), ("F", 2), ("T", 3), ("YF", 0), ("U", 3), ("ZS", 3), ("L", 4), ("A", 0, 2048, 2560),
    ("T", 4), ("M", 2), ("L", 2), ("U", 4), ("YS", 0), ("F", 5), ("A", 0, 2048, 3072), ("T", 2),
    ("L", 5), ("OF",), ("YS", 1), ("U", 2), ("A", 0, 2048, 2048), ("T", 5), ("U", 5), ("YS", 2),
    ("YF", 1),
)
TAIL = (
    ("OL",),
)
LAST_KEYS = 3584
LATE = (
    ("YL", 1), ("YF", 2), ("YL", 0), ("YF", 3), ("YL", 2), ("YL", 3),
)


def dot(a, b, ca, cb):
    return lax.dot_general(a, b, (((ca,), (cb,)), ((), ())), preferred_element_type=jnp.float32)


def modulate(tokens, mod_ref):
    values = tokens.astype(jnp.float32)
    mean = jnp.mean(values, axis=-1, keepdims=True)
    centred = values - mean
    var = jnp.mean(centred * centred, axis=-1, keepdims=True)
    normed = centred * lax.rsqrt(var + EPS)
    return (normed * (1.0 + mod_ref[1:2, :]) + mod_ref[0:1, :]).astype(jnp.bfloat16)


def kernel(
    hid_ref, mod_s_ref, mod_t_ref, ws_qkv_ref, ws_out_ref, wt_qkv_ref, wt_out_ref, out_ref,
    tok_a, tok_b, wsp, wso, wt, wto, q_buf, k_buf, v_buf, acc, top, o_send, o_recv,
    t_send, t_recv, r_send, heads_t, moved_t, send_sem, recv_sem,
):
    frame = lax.axis_index("frame")
    patch = lax.axis_index("patch")
    zlo, y = frame // 4, lax.rem(frame, 4)
    zhi, x, c = patch // 8, lax.rem(patch // 2, 4), lax.rem(patch, 2)
    z = zhi * 4 + zlo
    slot = x * 2 + c

    def device(z_=z, y_=y, x_=x, c_=c):
        return (lax.rem(z_, 4) * 4 + y_, (z_ // 4) * 8 + x_ * 2 + c_)

    def turn(value, step, size):
        return lax.rem(value + step + size, size)

    right, left = device(x_=turn(x, 1, 4)), device(x_=turn(x, -1, 4))
    sibling = device(c_=1 - c)
    partner = device(z_=turn(z, 4, 8))
    x_slots = [turn(x, d, 4) * 2 + c for d in range(4)]
    sib_slots = [turn(x, d, 4) * 2 + 1 - c for d in range(4)]

    barrier = pltpu.get_barrier_semaphore()
    greet = [device(x_=turn(x, d // 2, 4), c_=turn(c, d % 2, 2)) for d in range(1, 8)]
    greet += [(turn(frame, d, 16), patch) for d in range(1, 16)]
    greet += [device(z_=turn(z, d, 8)) for d in (4, 1, -1, 2, -2)]
    for other in greet:
        pl.semaphore_signal(barrier, inc=1, device_id=other, device_id_type=MESH)

    send_ids, recv_ids, fresh = {}, {}, [0]

    class Move:
        def __init__(self, src, dst, target, landing, group, recv_group=None):
            self.s = send_ids.setdefault(group, len(send_ids))
            if recv_group is None:
                fresh[0] += 1
                recv_group = fresh[0]
            self.r = recv_ids.setdefault(recv_group, len(recv_ids))
            self.src, self.dst, self.target, self.landing = src, dst, target, landing

        def start(self):
            pltpu.make_async_remote_copy(
                src_ref=self.src, dst_ref=self.dst, send_sem=send_sem.at[self.s],
                recv_sem=recv_sem.at[self.r], device_id=self.target, device_id_type=MESH,
            ).start()

        def wait_recv(self, landing=None):
            landing = self.landing if landing is None else landing
            pltpu.make_async_remote_copy(
                src_ref=landing, dst_ref=landing, send_sem=send_sem.at[self.s],
                recv_sem=recv_sem.at[self.r], device_id=self.target, device_id_type=MESH,
            ).wait_recv()

    def sent(group, ref):
        i = send_ids[group]
        pltpu.make_async_remote_copy(
            src_ref=ref, dst_ref=ref, send_sem=send_sem.at[i],
            recv_sem=recv_sem.at[0], device_id=sibling, device_id_type=MESH,
        ).wait_send()

    def start(*moves):
        for m in moves:
            m.start()

    def recv(*moves):
        for m in moves:
            m.wait_recv()

    class Ring:
        def __init__(self, buf, rows, cut, group, name):
            me, near, far, back = [buf.at[s] for s in x_slots]
            self.buf = buf
            self.to_right = Move(me, me, right, back, group)
            self.to_left = Move(me, me, left, near, group)
            top_half, low_half = pl.ds(0, cut), pl.ds(cut, rows - cut)
            self.on_right = Move(back.at[top_half], back.at[top_half], right, far.at[top_half], group)
            self.on_left = Move(near.at[low_half], near.at[low_half], left, far.at[low_half], group)
            self.sib = [
                Move(buf.at[x_slots[d]], buf.at[x_slots[d]], sibling, None, group, ("sib", name)) for d in range(4)
            ]

        def begin(self):
            start(self.to_right, self.to_left, self.sib[0])

        def forward(self):
            recv(self.to_right)
            start(self.on_right)
            recv(self.to_left)
            start(self.on_left, self.sib[3], self.sib[1])

        def last(self):
            recv(self.on_right, self.on_left)
            start(self.sib[2])

        def done(self):
            self.sib[0].wait_recv(self.buf.at[0:4])

    rings = [Ring(tok_a.at[n], 128, 64, "near", n) for n in range(2)]
    rings += [Ring(tok_b.at[n], 64, 32, "far", n + 2) for n in range(4)]
    to_partner = [
        Move(tok_a.at[n // 2, slot, pl.ds((n % 2) * 64, 64)], tok_b.at[n, slot], partner, tok_b.at[n, slot], "z")
        for n in range(4)
    ]
    wso_ring = Ring(wso, 144, 64, "wso", 6)

    edge = jnp.logical_or(zlo == 0, zlo == 3)
    ahead = jnp.where(zlo == 0, -1, 1)
    cross_src = wsp.at[0, y]
    cross_dst = wsp.at[1, y]
    cross_near = Move(cross_src, cross_dst, device(z_=turn(z, ahead, 8)), cross_dst, "c1", "cross")
    cross_far = Move(cross_src, cross_dst, device(z_=turn(z, 2 * ahead, 8)), cross_dst, "c2", "cross")
    share = [Move(cross_dst, cross_dst, device(y_=turn(y, d, 4)), None, "share", "share") for d in (1, 3, 2)]

    def wt_slot(dz, dy):
        return turn(zlo, dz, 4) * 4 + turn(y, dy, 4)

    def wt_half(dz, dy):
        return wt.at[wt_slot(dz, dy), c]

    two = jnp.where(c == 0, 2, -2)
    z_moves = [
        Move(wt_half(0, 0), wt_half(0, 0), device(z_=turn(z, 1, 8)), wt_half(-1, 0), "zw"),
        Move(wt_half(0, 0), wt_half(0, 0), device(z_=turn(z, -1, 8)), wt_half(1, 0), "zw"),
        Move(wt_half(0, 0), wt_half(0, 0), device(z_=turn(z, two, 8)), wt_half(2, 0), "zw"),
    ]
    y_up, y_down = device(y_=turn(y, 1, 4)), device(y_=turn(y, -1, 4))

    class YRing:
        def __init__(self, dz):
            me, near, far, back = [wt_half(dz, d) for d in range(4)]
            self.up = Move(me, me, y_up, back, "y")
            self.down = Move(me, me, y_down, near, "y")
            first, second = pl.ds(0, 64), pl.ds(64, 80)
            self.on_up = Move(back.at[first], back.at[first], y_up, far.at[first], "y")
            self.on_down = Move(near.at[second], near.at[second], y_down, far.at[second], "y")
            self.sib = [
                Move(wt_half(dz, d), wt_half(dz, d), sibling, None, "ysib", "ysib")
                for d in range(4) if (dz, d) != (0, 0)
            ]

        def begin(self):
            start(self.up, self.down)
            if len(self.sib) == 4:
                start(self.sib[0])

        def forward(self):
            recv(self.up)
            start(self.on_up)
            recv(self.down)
            start(self.on_down, self.sib[-1], self.sib[-3])

        def last(self):
            recv(self.on_up, self.on_down)
            start(self.sib[-2])

    y_rings = {dz: YRing(dz) for dz in Y_ORDER}

    def project(heads, ref, q_at, k_at):
        tokens = ref[...].reshape(-1, 1152)
        n = tokens.shape[0]
        for h in heads:
            qkv = dot(wsp[h].reshape(320, 1152)[0:224], tokens, 1, 1)
            if q_at is not None:
                q = jnp.concatenate([qkv[0:72] * Q_SCALE, jnp.zeros((8, n), jnp.float32)], axis=0)
                q_buf[h, :, pl.ds(q_at, n)] = q.astype(jnp.bfloat16)
            k = jnp.concatenate([qkv[72:144], jnp.zeros((8, n), jnp.float32)], axis=0)
            k_buf[h, pl.ds(k_at, n), :] = k.T.astype(jnp.bfloat16)
            row = lax.broadcasted_iota(jnp.int32, (8, n), 0)
            one = jnp.where(row == 0, 1.0, 0.0)
            v_buf[h, :, pl.ds(k_at, n)] = jnp.concatenate([qkv[144:216], one], axis=0).astype(jnp.bfloat16)

    def flash(h, q_at, q_n, k_at, k_n):
        qs, ks = pl.ds(q_at, q_n), pl.ds(k_at, k_n)
        s = dot(k_buf[h, ks, :], q_buf[h, :, qs], 1, 0)
        before = top[h, 0:1, qs]
        now = jnp.maximum(before, jnp.max(s, axis=0, keepdims=True))
        p = jnp.exp2(s - now).astype(jnp.bfloat16)
        acc[h, :, qs] = acc[h, :, qs] * jnp.exp2(before - now) + dot(v_buf[h, :, ks], p, 1, 0)
        top[h, 0:1, qs] = now

    moved = modulate(hid_ref[...], mod_s_ref)
    tok_a[0, slot] = moved[0:128]
    tok_a[1, slot] = moved[128:256]
    f32 = jnp.float32
    own = [ws_qkv_ref[...].astype(f32), ws_out_ref[...].astype(f32), jnp.zeros((32, 1152), f32)]
    wsp[0] = jnp.concatenate(own, axis=0).astype(jnp.bfloat16).reshape(4, 80, 1152)
    own = [wt_qkv_ref[...].astype(f32), wt_out_ref[...].astype(f32)]
    wt[frame] = jnp.concatenate(own, axis=0).astype(jnp.bfloat16).reshape(2, 144, 1152)
    acc[...] = jnp.zeros_like(acc)
    top[...] = jnp.full_like(top, LOW)
    pl.semaphore_wait(barrier, len(greet))

    def cross_start():
        @pl.when(edge)
        def _():
            cross_near.start()
            cross_far.start()

    def cross_share():
        recv(cross_near)
        start(*share)

    def share_done():
        share[0].wait_recv(wsp.at[1, 0:3])
        rows = [wsp[h].reshape(320, 1152)[208:288].astype(jnp.float32)[8:80] for h in range(2)]
        wso[slot] = jnp.concatenate(rows, axis=0).astype(jnp.bfloat16)

    def forward_z(n):
        recv(to_partner[n])
        rings[n + 2].begin()

    def forward_y(i):
        recv(z_moves[i])
        y_rings[Y_ORDER[i + 1]].begin()

    def tokens_done(n):
        rings[n].done()
        project((0,), *chunks[n])

    def attend(q_at, q_n, k_at):
        for h in range(2):
            flash(h, q_at, q_n, k_at, 512)

    chunks = [(tok_a.at[n], n * 1024, n * 1024) for n in range(2)]
    chunks += [(tok_b.at[n], None, 2048 + n * 512) for n in range(4)]
    steps = {
        "S": lambda n: rings[n].begin(),
        "F": lambda n: rings[n].forward(),
        "L": lambda n: rings[n].last(),
        "T": tokens_done,
        "U": lambda n: project((1,), *chunks[n]),
        "A": attend,
        "Z": lambda n: to_partner[n].start(),
        "ZS": forward_z,
        "C": cross_start,
        "CS": cross_share,
        "CD": share_done,
        "M": lambda i: z_moves[i].start(),
        "Y": lambda: y_rings[0].begin(),
        "YS": forward_y,
        "YF": lambda i: y_rings[Y_ORDER[i]].forward(),
        "YL": lambda i: y_rings[Y_ORDER[i]].last(),
        "YD": lambda i: y_rings[Y_ORDER[i]].done(),
        "OS": lambda: wso_ring.begin(),
        "OF": lambda: wso_ring.forward(),
        "OL": lambda: wso_ring.last(),
    }
    for step in SCHEDULE:
        steps[step[0]](*step[1:])

    def heads_back(n):
        attend(n * 1024, 1024, LAST_KEYS)
        for s in range(8):
            pair = []
            for h in range(2):
                part = acc[h, :, pl.ds(n * 1024 + s * 128, 128)]
                pair.append(part[0:72] * (1.0 / part[72:73]))
            o_send[n, s] = jnp.concatenate(pair, axis=0).astype(jnp.bfloat16)
        moves = []
        for d in range(1, 8):
            to = turn(x, d // 2, 4) * 2 + turn(c, d % 2, 2)
            target = device(x_=to // 2, c_=lax.rem(to, 2))
            moves.append(Move(o_send.at[n, to], o_recv.at[n, slot], target, None, "o", ("o", n)))
        start(*moves)
        o_recv[n, slot] = o_send[n, slot]
        return moves

    my_rows = y * 4 + zlo

    def spatial_end(n, moves):
        moves[0].wait_recv(o_recv.at[n, 0:7])
        update = dot(o_recv[n].reshape(1152, 128), wso[...].reshape(1152, 1152), 0, 0)
        old = hid_ref[pl.ds(n * 128, 128), :].astype(f32)
        after = (old + mod_s_ref[2:3, :] * update).astype(jnp.bfloat16)
        t_send[pl.ds(8 * n, 8)] = after.reshape(8, 16, 1152)
        moves = []
        for dz in (2, 1, 3, 0):
            for to_y in (2 * n, 2 * n + 1):
                to_z = turn(zlo, dz, 4)
                move = Move(
                    t_send.at[4 * to_y + to_z], t_recv.at[frame], (4 * to_z + to_y, patch), None, "there", "there"
                )
                if dz == 0:
                    pl.when(y != to_y)(move.start)
                else:
                    move.start()
                moves.append(move)
        return moves

    first = heads_back(0)
    second = heads_back(1)
    for step in TAIL:
        steps[step[0]](*step[1:])
    wso_ring.done()
    there = spatial_end(0, first)
    spatial_end(1, second)

    t_recv[frame] = t_send[my_rows]
    for step in LATE:
        steps[step[0]](*step[1:])
    there[0].wait_recv(t_recv.at[0:15])
    tokens = t_recv[...].reshape(256, 1152)
    t_moved = modulate(tokens, mod_t_ref)
    key = lax.rem(lax.broadcasted_iota(jnp.int32, (256, 256), 0), 16)
    query = lax.rem(lax.broadcasted_iota(jnp.int32, (256, 256), 1), 16)
    bias = jnp.where(key == query, 0.0, LOW)
    one = jnp.where(lax.broadcasted_iota(jnp.int32, (8, 256), 0) == 0, 1.0, 0.0)
    moved_t[...] = t_moved.astype(f32).T.astype(jnp.bfloat16)

    y_rings[0].sib[0].wait_recv(wt.at[0:15, 0])

    def four_heads(g, _):
        for j in range(2):
            rows = [wt[4 * g + 2 * j + k].reshape(288, 1152)[208:288].astype(f32)[8:80] for k in range(2)]
            wto[2 * g + j] = jnp.concatenate(rows, axis=0).astype(jnp.bfloat16)
        qkv = dot(wt[pl.ds(4 * g, 4)].reshape(1152, 1152), moved_t[...], 1, 0)
        for i in range(4):
            part = qkv[288 * i:288 * i + 216]
            q = (part[0:72] * Q_SCALE).astype(jnp.bfloat16)
            k = part[72:144].T.astype(jnp.bfloat16)
            v = jnp.concatenate([part[144:216], one], axis=0).astype(jnp.bfloat16)
            s = dot(k, q, 1, 0) + bias
            p = jnp.exp2(s - jnp.max(s, axis=0, keepdims=True)).astype(jnp.bfloat16)
            o = dot(v, p, 1, 0)
            rows = pl.ds(pl.multiple_of((4 * g + i) * 72, 8), 72)
            heads_t[rows, :] = o[0:72] * (1.0 / o[72:73])
        return 0

    lax.fori_loop(0, 4, four_heads, 0)
    update = dot(heads_t[...].astype(jnp.bfloat16), wto[...].reshape(1152, 1152), 0, 0)
    block = tokens.astype(jnp.float32) + mod_t_ref[2:3, :] * update
    r_send[...] = block.astype(jnp.bfloat16).reshape(16, 16, 1152)
    back = []
    for d in range(1, 16):
        to = turn(frame, d, 16)
        back.append(Move(r_send.at[to], out_ref.at[my_rows], (to, patch), None, "back", "back"))
    start(*back)
    out_ref[my_rows] = r_send[frame]
    back[0].wait_recv(out_ref.at[0:15])

    sent("near", tok_b.at[0:4, 0:7])
    sent("far", tok_b.at[0:4, 0:7])
    sent("wso", wso.at[0:7])
    sent("z", tok_b.at[0, 0:4])
    sent("share", wsp.at[1, 0:3])
    sent("zw", wso.at[0:3])
    sent("y", wt.at[0:6])
    sent("ysib", wt.at[0:15, 0])
    sent("o", o_recv.at[0:2, 0:7])
    sent("there", t_recv.at[0:15])
    sent("back", t_recv.at[0:15])

    @pl.when(edge)
    def _():
        sent("c1", cross_src)
        sent("c2", cross_src)

    assert len(send_ids) <= N_SEND and len(recv_ids) <= N_RECV


def shards(hidden, mod_s, w_s_qkv, w_s_out, mod_t, w_t_qkv, w_t_out):
    vmem = pl.BlockSpec(memory_space=pltpu.VMEM)
    bf, f32 = jnp.bfloat16, jnp.float32
    out = pl.pallas_call(
        kernel,
        out_shape=jax.ShapeDtypeStruct((16, 16, 1152), bf),
        in_specs=[vmem] * 7,
        out_specs=vmem,
        scratch_shapes=[
            pltpu.VMEM((2, 8, 128, 1152), bf),
            pltpu.VMEM((4, 8, 64, 1152), bf),
            pltpu.VMEM((2, 4, 80, 1152), bf),
            pltpu.VMEM((8, 144, 1152), bf),
            pltpu.VMEM((16, 2, 144, 1152), bf),
            pltpu.VMEM((8, 144, 1152), bf),
            pltpu.VMEM((2, 80, 2048), bf),
            pltpu.VMEM((2, 4096, 80), bf),
            pltpu.VMEM((2, 80, 4096), bf),
            pltpu.VMEM((2, 80, 2048), f32),
            pltpu.VMEM((2, 8, 2048), f32),
            pltpu.VMEM((2, 8, 144, 128), bf),
            pltpu.VMEM((2, 8, 144, 128), bf),
            pltpu.VMEM((16, 16, 1152), bf),
            pltpu.VMEM((16, 16, 1152), bf),
            pltpu.VMEM((16, 16, 1152), bf),
            pltpu.VMEM((1152, 256), f32),
            pltpu.VMEM((1152, 256), bf),
            pltpu.SemaphoreType.DMA((N_SEND,)),
            pltpu.SemaphoreType.DMA((N_RECV,)),
        ],
        compiler_params=pltpu.CompilerParams(
            collective_id=0, has_side_effects=True, vmem_limit_bytes=62 * 2**20
        ),
        name="st_block",
    )(hidden.reshape(256, 1152), mod_s, mod_t, w_s_qkv.T, w_s_out, w_t_qkv.T, w_t_out)
    return out.reshape(1, 256, 1152)


def solution(mesh):
    in_specs = (
        P("frame", "patch", None),
        P(),
        P(None, "patch"),
        P("patch", None),
        P(),
        P(None, "frame"),
        P("frame", None),
    )
    out_specs = P("frame", "patch", None)
    return jax.shard_map(shards, mesh=mesh, in_specs=in_specs, out_specs=out_specs, check_vma=False)
```
